512 devices in a mesh: pair: 32 (over z, x_lo), row: 16 (over y, x_hi, core).
Axes of the slice: x: 4 (x_hi: 2, x_lo: 2; x = x_hi * 2 + x_lo), y: 4, z: 16, core: 2. Of those that a mesh axis runs over, the one named last changes fastest.
Arguments:
- matrix: float32 [65536, 4096], P('row', 'pair'), may hold values from -60 to 60, as said below
- stay_side: int32 [4, 32], P(None, 'pair'), may hold values from 0 to 1
Outputs:
- rotated: float32 [65536, 4096], P('row', 'pair')
The draws below stay inside these ranges and needn't reach their ends.
Inputs may be any that keep to these rules, and one draw needn't show every extreme that they name: `matrix`: entries are real-valued and of mixed magnitude.
All inputs are finite; a program needn't handle non-finite values.
Results may differ from the reference program's by a relative error of at most 0.0003.
Values sent between devices are 32-bit elements; how exact they have to be, the bound alone decides.
No kernel may reach another device: no remote copies, remote signals or barrier semaphores. Data moves between devices by JAX's collectives and lax.ppermute only.
A program may use at most 64 MiB of HBM per device.

```python
import math
import jax
import jax.numpy as jnp
from jax import lax

BW = 64
ROUNDS = 4
NS_STEPS = 6
COLS = 4096
ROWS = 65536
N_PAIR = 32


def draw_matrix(key, part):
    key = jax.random.fold_in(key, 11)
    first_key, second_key = jax.random.split(key, 2)
    noise = jax.random.truncated_normal(first_key, -4.0, 4.0, (ROWS, COLS), jnp.float32)
    rough = noise + 0.5 * jnp.roll(noise, -1, axis=1)
    scales = jnp.exp(jax.random.uniform(second_key, (COLS,), jnp.float32, 0.0, math.log(10.0)))
    return (rough * scales[None, :]).astype(jnp.float32)


def set_ends(values, stream_key, least, largest):
    longest = values.shape.index(max(values.shape))
    spots = []
    for shift in (0, 1):
        where = [jax.random.randint(jax.random.fold_in(stream_key, axis), (), 0, length) for axis, length in enumerate(values.shape)]
        where[longest] = (where[longest] + shift) % values.shape[longest]
        spots.append(tuple(where))
    return values.at[spots[0]].set(least).at[spots[1]].set(largest)


def setup_inputs(seed: int = 0) -> dict:
    arg_keys = jax.random.split(jax.random.key(seed), 3)
    return {
        "matrix": draw_matrix(jax.random.fold_in(arg_keys[2], 71), 0),
        "stay_side": set_ends(jax.random.randint(arg_keys[1], (ROUNDS, N_PAIR), 0, 2), jax.random.fold_in(arg_keys[1], 1), 0, 1).astype(jnp.int32),
    }


def newton_schulz(gram):
    order = gram.shape[0]
    scale = jnp.sqrt(jnp.sum(gram * gram) + 1e-06)
    ident = jnp.eye(order, dtype=jnp.float32)
    ymat = gram / scale
    zmat = ident
    for step in range(NS_STEPS):
        stepper = 1.5 * ident - 0.5 * jnp.dot(zmat, ymat, precision=lax.Precision.HIGHEST)
        ymat = jnp.dot(ymat, stepper, precision=lax.Precision.HIGHEST)
        zmat = jnp.dot(stepper, zmat, precision=lax.Precision.HIGHEST)
    return (zmat, scale)

def one_pair(inputs):
    slab, side = inputs
    gram = jnp.dot(slab.T, slab, precision=lax.Precision.HIGHEST)
    zmat, scale = newton_schulz(gram)
    newer = jnp.dot(slab, zmat, precision=lax.Precision.HIGHEST) * jnp.sqrt(ROWS / scale)
    first = newer[:, :BW]
    second = newer[:, BW:]
    stay = jnp.where(side == 0, first, second)
    move = jnp.where(side == 0, second, first)
    return (stay, move)

def reference(matrix, stay_side):
    pairs = matrix.shape[1] // (2 * BW)
    current = matrix.reshape(ROWS, pairs, 2 * BW).transpose(1, 0, 2)
    for round_index in range(ROUNDS):
        stay, move = lax.map(one_pair, (current, stay_side[round_index]))
        arrived = jnp.roll(move, 1, axis=0)
        current = jnp.concatenate([stay, arrived], axis=2)
    return current.transpose(1, 0, 2).reshape(ROWS, pairs * 2 * BW)
```

```python
import jax
import jax.numpy as jnp
from jax import lax
from jax.sharding import PartitionSpec as P

ROUNDS = 4
NS_STEPS = 6


def passed_along(shard, axis, by):
    peers = lax.axis_size(axis)
    return lax.ppermute(shard, axis, [(i, (i + by) % peers) for i in range(peers)])


def newton_schulz(gram):
    order = gram.shape[0]
    scale = jnp.sqrt(jnp.sum(gram * gram) + 1e-06)
    ident = jnp.eye(order, dtype=jnp.float32)
    ymat = gram / scale
    zmat = ident
    for step in range(NS_STEPS):
        stepper = 1.5 * ident - 0.5 * jnp.dot(zmat, ymat, precision=lax.Precision.HIGHEST)
        ymat = jnp.dot(ymat, stepper, precision=lax.Precision.HIGHEST)
        zmat = jnp.dot(stepper, zmat, precision=lax.Precision.HIGHEST)
    return (zmat, scale)


def row_sum(part):
    peers = lax.axis_size("row")
    part = part + lax.ppermute(part, "row", [(i, i ^ 1) for i in range(peers)])
    same_core = [[core + 2 * chip for chip in range(peers // 2)] for core in range(2)]
    copies = jnp.broadcast_to(part[None], (peers // 2,) + part.shape)
    gathered = lax.all_to_all(copies, "row", 0, 0, axis_index_groups=same_core)
    return jnp.sum(gathered, axis=0)


def full_gram(slab):
    local_gram = jnp.dot(slab.T, slab, precision=lax.Precision.HIGHEST)
    return row_sum(local_gram)


def shift_block(move):
    return passed_along(move, "pair", 1)


def local(matrix, stay_side):
    width = matrix.shape[1] // 2
    total_rows = matrix.shape[0] * lax.axis_size("row")
    current = matrix
    stay = matrix[:, :width]
    arrived = matrix[:, width:]
    for round_index in range(ROUNDS):
        side = stay_side[round_index, 0]
        if round_index == 0:
            gram = full_gram(current)
        else:
            gram = full_gram(current)
        zmat, scale = newton_schulz(gram)
        factor = jnp.sqrt(total_rows / scale)
        newer = jnp.dot(current, zmat, precision=lax.Precision.HIGHEST) * factor
        stay = jnp.where(side == 0, newer[:, :width], newer[:, width:])
        move = jnp.where(side == 0, newer[:, width:], newer[:, :width])
        if round_index + 1 == ROUNDS:
            arrived = shift_block(move)
        else:
            arrived = shift_block(move)
        current = jnp.concatenate([stay, arrived], axis=1)
    return current


def solution(mesh):
    return jax.shard_map(
        local,
        mesh=mesh,
        in_specs=(P("row", "pair"), P(None, "pair")),
        out_specs=P("row", "pair"),
        check_vma=False,
    )
```

```python
import jax
import jax.numpy as jnp
from jax import lax
from jax.sharding import PartitionSpec as P

ROUNDS = 4
NS_STEPS = 6
HIGHEST = lax.Precision.HIGHEST


def passed_along(shard, axis, by):
    peers = lax.axis_size(axis)
    return lax.ppermute(shard, axis, [(i, (i + by) % peers) for i in range(peers)])


def newton_schulz(gram):
    order = gram.shape[0]
    scale = jnp.sqrt(jnp.sum(gram * gram) + 1e-06)
    ident = jnp.eye(order, dtype=jnp.float32)
    ymat = gram / scale
    zmat = ident
    for step in range(NS_STEPS):
        stepper = 1.5 * ident - 0.5 * jnp.dot(zmat, ymat, precision=HIGHEST)
        if step + 1 < NS_STEPS:
            ymat = jnp.dot(ymat, stepper, precision=HIGHEST)
        zmat = jnp.dot(stepper, zmat, precision=HIGHEST)
    return (zmat, scale)


def row_sum(part):
    peers = lax.axis_size("row")
    part = part + lax.ppermute(part, "row", [(i, i ^ 1) for i in range(peers)])
    same_core = [[core + 2 * chip for chip in range(peers // 2)] for core in range(2)]
    copies = jnp.broadcast_to(part[None], (peers // 2,) + part.shape)
    gathered = lax.all_to_all(copies, "row", 0, 0, axis_index_groups=same_core)
    return jnp.sum(gathered, axis=0)


def local(matrix, stay_side):
    width = matrix.shape[1] // 2
    total_rows = matrix.shape[0] * lax.axis_size("row")
    mine = matrix
    before = passed_along(matrix, "pair", 1)
    for round_index in range(ROUNDS):
        last = round_index + 1 == ROUNDS
        gram = row_sum(jnp.dot(mine.T, mine, precision=HIGHEST))
        zmat, scale = newton_schulz(gram)
        turn = zmat * jnp.sqrt(total_rows / scale)
        side = stay_side[round_index, 0]
        turn = jnp.where(side == 0, turn, jnp.concatenate([turn[:, width:], turn[:, :width]], axis=1))
        if last:
            turn_before = passed_along(turn[:, width:], "pair", 1)
        else:
            turn_before = passed_along(turn, "pair", 1)
        stay = jnp.dot(mine, turn[:, :width], precision=HIGHEST)
        moved = jnp.dot(before, turn_before, precision=HIGHEST)
        if last:
            return jnp.concatenate([stay, moved], axis=1)
        arrived = moved[:, width:]
        mine = jnp.concatenate([stay, arrived], axis=1)
        before = jnp.concatenate([moved[:, :width], passed_along(arrived, "pair", 1)], axis=1)


def solution(mesh):
    return jax.shard_map(
        local,
        mesh=mesh,
        in_specs=(P("row", "pair"), P(None, "pair")),
        out_specs=P("row", "pair"),
        check_vma=False,
    )
```

```python
import functools

import jax
import jax.numpy as jnp
from jax import lax
from jax.experimental import pallas as pl
from jax.experimental.pallas import tpu as pltpu
from jax.sharding import PartitionSpec as P

ROUNDS = 4
NS_STEPS = 6
HIGHEST = lax.Precision.HIGHEST


def mul(a, b):
    return jnp.dot(a, b, precision=HIGHEST)


def passed_along(shard, axis, by):
    peers = lax.axis_size(axis)
    return lax.ppermute(shard, axis, [(i, (i + by) % peers) for i in range(peers)])


def turn_kernel(total_rows, cross, side_ref, sums_ref, *refs):
    if cross:
        gram_stay_ref, gram_arrived_ref, gram_ref, turn_ref = refs
    else:
        gram_ref, turn_ref = refs
    order = gram_ref.shape[0]
    width = order // 2
    total = sums_ref[0]
    for device in range(1, sums_ref.shape[0]):
        total = total + sums_ref[device]
    if cross:
        block = jnp.concatenate([total[:, :width], total[:, width:]], axis=0)
        gram_ref[:width, :width] = gram_stay_ref[...]
        gram_ref[:width, width:] = block
        gram_ref[width:, :width] = block.T
        gram_ref[width:, width:] = gram_arrived_ref[...]
    else:
        gram_ref[:width, :] = total[:width]
        gram_ref[width:, :width] = total[:width, width:].T
        gram_ref[width:, width:] = jnp.concatenate([total[width:, :width], total[width:, width:]], axis=0)
    gram = gram_ref[...]
    scale = jnp.sqrt(jnp.sum(gram * gram) + 1e-06)
    down = lax.broadcasted_iota(jnp.int32, (order, order), 0)
    along = lax.broadcasted_iota(jnp.int32, (order, order), 1)
    half_more = jnp.where(down == along, 1.5, 0.0).astype(jnp.float32)
    ymat = gram / scale
    stepper = half_more - 0.5 * ymat
    both = jnp.concatenate([mul(stepper, ymat), stepper], axis=1)
    for step in range(1, NS_STEPS):
        ymat, zmat = both[:, :order], both[:, order:]
        stepper = half_more - 0.5 * mul(zmat, ymat)
        if step + 1 < NS_STEPS:
            both = mul(stepper, both)
        else:
            zmat = mul(stepper, zmat)
    zmat = zmat * jnp.sqrt(total_rows / scale)
    swapped = pltpu.roll(zmat, width, 1)
    turn_ref[...] = jnp.where(side_ref[0] == 0, zmat, swapped)


def turned(sums, side, total_rows, blocks=()):
    order = sums.shape[-1]
    square = jax.ShapeDtypeStruct((order, order), jnp.float32)
    in_vmem = pl.BlockSpec(memory_space=pltpu.VMEM)
    return pl.pallas_call(
        functools.partial(turn_kernel, total_rows, bool(blocks)),
        out_shape=(square, square),
        in_specs=[pl.BlockSpec(memory_space=pltpu.SMEM)] + [in_vmem] * (1 + len(blocks)),
        out_specs=(in_vmem, in_vmem),
        compiler_params=pltpu.CompilerParams(vmem_limit_bytes=3 << 20),
        cost_estimate=pl.CostEstimate(flops=200_000_000, bytes_accessed=500_000, transcendentals=0),
    )(side, sums, *blocks)


def shares(part, over_cores):
    peers = lax.axis_size("row")
    groups = None
    if over_cores:
        part = part + lax.ppermute(part, "row", [(i, i ^ 1) for i in range(peers)])
        groups = [[core + 2 * chip for chip in range(peers // 2)] for core in range(2)]
        peers = peers // 2
    copies = jnp.broadcast_to(part[None], (peers,) + part.shape)
    return lax.all_to_all(copies, "row", 0, 0, axis_index_groups=groups)


def folded(block):
    half = block.shape[0] // 2
    return jnp.concatenate([block[:half], block[half:]], axis=1)


def gram_shares(stay, arrived):
    slab = jnp.concatenate([stay, arrived], axis=1)
    width = stay.shape[1]
    part = mul(slab.T, slab)
    return shares(jnp.concatenate([part[:width], folded(part[width:, width:])], axis=0), True)


def local(matrix, stay_side):
    rows, width = matrix.shape[0], matrix.shape[1] // 2
    total_rows = float(rows * lax.axis_size("row"))
    stay, arrived = matrix[:, :width], matrix[:, width:]
    gram, turn = turned(gram_shares(stay, arrived), stay_side[0], total_rows)
    for round_index in range(ROUNDS):
        following = round_index + 1
        current = jnp.concatenate([stay, arrived], axis=1)
        to_stay, to_move = turn[:, :width], turn[:, width:]
        arrived = passed_along(mul(current, to_move), "pair", 1)
        stay = mul(current, to_stay)
        if following == ROUNDS:
            return jnp.concatenate([stay, arrived], axis=1)
        if following % 2 == 0:
            gram, turn = turned(gram_shares(stay, arrived), stay_side[following], total_rows)
        else:
            gram_stay = mul(to_stay.T, mul(gram, to_stay))
            gram_arrived = passed_along(mul(to_move.T, mul(gram, to_move)), "pair", 1)
            cross = shares(folded(mul(stay.T, arrived)), False)
            gram, turn = turned(cross, stay_side[following], total_rows, (gram_stay, gram_arrived))


def solution(mesh):
    return jax.shard_map(
        local,
        mesh=mesh,
        in_specs=(P("row", "pair"), P(None, "pair")),
        out_specs=P("row", "pair"),
        check_vma=False,
    )
```

```python
import functools

import jax
import jax.numpy as jnp
from jax import lax
from jax.experimental import pallas as pl
from jax.experimental.pallas import tpu as pltpu
from jax.sharding import PartitionSpec as P

ROUNDS = 4
NS_STEPS = 6
HIGHEST = lax.Precision.HIGHEST
IN_VMEM = pl.BlockSpec(memory_space=pltpu.VMEM)


def mul(a, b):
    return jnp.dot(a, b, precision=HIGHEST)


def terms(x):
    first = x.astype(jnp.bfloat16)
    rest = x - first.astype(jnp.float32)
    second = rest.astype(jnp.bfloat16)
    third = (rest - second.astype(jnp.float32)).astype(jnp.bfloat16)
    return first, second, third


def mul_terms(a, b):
    left = jnp.concatenate([a[0], a[0], a[0], a[1], a[1], a[2]], axis=1)
    right = jnp.concatenate([b[0], b[1], b[2], b[0], b[1], b[0]], axis=0)
    return jnp.dot(left, right, preferred_element_type=jnp.float32)


def added_up(products, height, width):
    block = lambda i, j: products[i * height : (i + 1) * height, j * width : (j + 1) * width]
    small = (block(2, 2) + (block(1, 2) + block(2, 1))) + (block(0, 2) + block(2, 0) + block(1, 1))
    return small + (block(0, 1) + block(1, 0)) + block(0, 0)


def passed_along(shard, axis, by):
    peers = lax.axis_size(axis)
    return lax.ppermute(shard, axis, [(i, (i + by) % peers) for i in range(peers)])


def turn_kernel(total_rows, cross, side_ref, sums_ref, *refs):
    if cross:
        gram_stay_ref, gram_arrived_ref, gram_ref, turn_ref = refs
    else:
        gram_ref, turn_ref = refs
    order = gram_ref.shape[0]
    width = order // 2
    total = sums_ref[0]
    for device in range(1, sums_ref.shape[0]):
        total = total + sums_ref[device]
    if cross:
        block = jnp.concatenate([total[:, :width], total[:, width:]], axis=0)
        gram_ref[:width, :width] = gram_stay_ref[...]
        gram_ref[:width, width:] = block
        gram_ref[width:, :width] = block.T
        gram_ref[width:, width:] = gram_arrived_ref[...]
    else:
        gram_ref[:width, :] = total[:width]
        gram_ref[width:, :width] = total[:width, width:].T
        gram_ref[width:, width:] = jnp.concatenate([total[width:, :width], total[width:, width:]], axis=0)
    gram = gram_ref[...]
    scale = jnp.sqrt(jnp.sum(gram * gram) + 1e-06)
    down = lax.broadcasted_iota(jnp.int32, (order, order), 0)
    along = lax.broadcasted_iota(jnp.int32, (order, order), 1)
    half_more = jnp.where(down == along, 1.5, 0.0).astype(jnp.float32)
    ymat = gram / scale
    stepper = half_more - 0.5 * ymat
    beside = lambda y, z: [jnp.concatenate(pair, axis=1) for pair in zip(y, z)]
    z_terms = terms(stepper)
    y_terms = terms(mul_terms(z_terms, terms(ymat)))
    for step in range(1, NS_STEPS):
        stepper = half_more - 0.5 * mul_terms(z_terms, y_terms)
        if step + 1 < NS_STEPS:
            both = mul_terms(terms(stepper), beside(y_terms, z_terms))
            y_terms, z_terms = terms(both[:, :order]), terms(both[:, order:])
        else:
            zmat = mul_terms(terms(stepper), z_terms)
    zmat = zmat * jnp.sqrt(total_rows / scale)
    swapped = pltpu.roll(zmat, width, 0)
    turn_ref[...] = jnp.where(side_ref[0] == 0, zmat, swapped)


def turned(sums, side, total_rows, blocks=()):
    order = sums.shape[-1]
    square = jax.ShapeDtypeStruct((order, order), jnp.float32)
    return pl.pallas_call(
        functools.partial(turn_kernel, total_rows, bool(blocks)),
        out_shape=(square, square),
        in_specs=[pl.BlockSpec(memory_space=pltpu.SMEM)] + [IN_VMEM] * (1 + len(blocks)),
        out_specs=(IN_VMEM, IN_VMEM),
        compiler_params=pltpu.CompilerParams(vmem_limit_bytes=4 << 20),
        cost_estimate=pl.CostEstimate(flops=200_000_000, bytes_accessed=500_000, transcendentals=0),
    )(side, sums, *blocks)


def shares(copies):
    return lax.all_to_all(copies, "row", 0, 0)


def shares_of_chips(part):
    peers = lax.axis_size("row")
    part = part + lax.ppermute(part, "row", [(i, i ^ 1) for i in range(peers)])
    groups = [[core + 2 * chip for chip in range(peers // 2)] for core in range(2)]
    copies = jnp.broadcast_to(part[None], (peers // 2,) + part.shape)
    return lax.all_to_all(copies, "row", 0, 0, axis_index_groups=groups)


def folded(block):
    half = block.shape[0] // 2
    return jnp.concatenate([block[:half], block[half:]], axis=1)


def packed_gram(gram):
    width = gram.shape[0] // 2
    return jnp.concatenate([gram[:width], folded(gram[width:, width:])], axis=0)


def mul_nt(a, b):
    return lax.dot_general(a, b, (((1,), (1,)), ((), ())), precision=HIGHEST, preferred_element_type=jnp.float32)


def entry_kernel(x_ref, xt_ref, part_ref):
    pieces = 8
    height = x_ref.shape[0] // pieces
    gram = None
    for piece in range(pieces):
        slab = x_ref[piece * height : (piece + 1) * height, :]
        turned_over = slab.T
        xt_ref[:, piece * height : (piece + 1) * height] = turned_over
        product = jnp.dot(
            jnp.concatenate(terms(turned_over), axis=0),
            jnp.concatenate(terms(slab), axis=1),
            preferred_element_type=jnp.float32,
        )
        gram = product if gram is None else gram + product
    part_ref[...] = packed_gram(added_up(gram, gram.shape[0] // 3, gram.shape[1] // 3))


def entry(matrix):
    rows, order = matrix.shape
    return pl.pallas_call(
        entry_kernel,
        out_shape=(
            jax.ShapeDtypeStruct((order, rows), jnp.float32),
            jax.ShapeDtypeStruct((3 * order // 4, order), jnp.float32),
        ),
        in_specs=[IN_VMEM],
        out_specs=(IN_VMEM, IN_VMEM),
        compiler_params=pltpu.CompilerParams(vmem_limit_bytes=10 << 20),
        cost_estimate=pl.CostEstimate(flops=800_000_000, bytes_accessed=4_000_000, transcendentals=0),
    )(matrix)


def gram_kernel(stay_ref, arrived_ref, part_ref):
    rows = stay_ref.shape[1]
    whole = len(part_ref.shape) == 2
    pieces = 4
    length = rows // pieces
    gram = None
    for piece in range(pieces):
        where = slice(piece * length, (piece + 1) * length)
        left, right = stay_ref[:, where], arrived_ref[:, where]
        if whole:
            left = right = jnp.concatenate([left, right], axis=0)
        left = jnp.concatenate(terms(left), axis=0)
        right = left if whole else jnp.concatenate(terms(right), axis=0)
        product = lax.dot_general(left, right, (((1,), (1,)), ((), ())), preferred_element_type=jnp.float32)
        gram = product if gram is None else gram + product
    gram = added_up(gram, gram.shape[0] // 3, gram.shape[1] // 3)
    if whole:
        part_ref[...] = packed_gram(gram)
    else:
        packed = folded(gram)
        for device in range(part_ref.shape[0]):
            part_ref[device] = packed


def gram_part(stay, arrived, copies=None):
    width = stay.shape[0]
    shape = (3 * width // 2, 2 * width) if copies is None else (copies, width // 2, 2 * width)
    return pl.pallas_call(
        gram_kernel,
        out_shape=jax.ShapeDtypeStruct(shape, jnp.float32),
        in_specs=[IN_VMEM, IN_VMEM],
        out_specs=IN_VMEM,
        compiler_params=pltpu.CompilerParams(vmem_limit_bytes=8 << 20),
        cost_estimate=pl.CostEstimate(flops=400_000_000, bytes_accessed=3_000_000, transcendentals=0),
    )(stay, arrived)


def exit_kernel(stay_ref, arrived_ref, out_ref, held_ref, sems):
    pieces = sems.shape[0]
    height = out_ref.shape[0] // pieces
    copies = []
    for piece in range(pieces):
        where = slice(piece * height, (piece + 1) * height)
        held_ref[where, :] = jnp.concatenate([stay_ref[:, where], arrived_ref[:, where]], axis=0).T
        rows = pl.ds(piece * height, height)
        copy = pltpu.make_async_copy(held_ref.at[rows], out_ref.at[rows], sems.at[piece])
        copy.start()
        copies.append(copy)
    for copy in copies:
        copy.wait()


def assembled(stay, arrived):
    width, rows = stay.shape
    pieces = 8
    return pl.pallas_call(
        exit_kernel,
        out_shape=jax.ShapeDtypeStruct((rows, 2 * width), jnp.float32),
        in_specs=[IN_VMEM, IN_VMEM],
        out_specs=pl.BlockSpec(memory_space=pltpu.HBM),
        scratch_shapes=[pltpu.VMEM((rows, 2 * width), jnp.float32), pltpu.SemaphoreType.DMA((pieces,))],
        compiler_params=pltpu.CompilerParams(vmem_limit_bytes=8 << 20),
        cost_estimate=pl.CostEstimate(flops=0, bytes_accessed=4_000_000, transcendentals=0),
    )(stay, arrived)


def local(matrix, stay_side):
    rows, width = matrix.shape[0], matrix.shape[1] // 2
    total_rows = float(rows * lax.axis_size("row"))
    peers = lax.axis_size("row")
    current, part = entry(matrix)
    gram, turn = turned(shares_of_chips(part), stay_side[0], total_rows)
    for round_index in range(ROUNDS):
        following = round_index + 1
        to_stay, to_move = turn[:width], turn[width:]
        arrived = passed_along(mul(to_move, current), "pair", 1)
        stay = mul(to_stay, current)
        if following == ROUNDS:
            return assembled(stay, arrived)
        current = jnp.concatenate([stay, arrived], axis=0)
        if following % 2 == 0:
            gram, turn = turned(shares_of_chips(gram_part(stay, arrived)), stay_side[following], total_rows)
        else:
            gram_stay = mul_nt(mul(to_stay, gram), to_stay)
            gram_arrived = passed_along(mul_nt(mul(to_move, gram), to_move), "pair", 1)
            arrived, gram_arrived = lax.optimization_barrier((arrived, gram_arrived))
            current = jnp.concatenate([stay, arrived], axis=0)
            copies = gram_part(stay, arrived, peers)
            gram, turn = turned(shares(copies), stay_side[following], total_rows, (gram_stay, gram_arrived))


def solution(mesh):
    return jax.shard_map(
        local,
        mesh=mesh,
        in_specs=(P("row", "pair"), P(None, "pair")),
        out_specs=P("row", "pair"),
        check_vma=False,
    )
```

```python
import functools

import jax
import jax.numpy as jnp
from jax import lax
from jax.experimental import pallas as pl
from jax.experimental.pallas import tpu as pltpu
from jax.sharding import PartitionSpec as P

ROUNDS = 4
NS_STEPS = 6
GROUPS = 2
HIGHEST = lax.Precision.HIGHEST
IN_VMEM = pl.BlockSpec(memory_space=pltpu.VMEM)


def mul(a, b):
    return jnp.dot(a, b, precision=HIGHEST)


def terms(x):
    first = x.astype(jnp.bfloat16)
    rest = x - first.astype(jnp.float32)
    second = rest.astype(jnp.bfloat16)
    third = (rest - second.astype(jnp.float32)).astype(jnp.bfloat16)
    return first, second, third


def mul_terms(a, b):
    left = jnp.concatenate([a[0], a[0], a[0], a[1], a[1], a[2]], axis=1)
    right = jnp.concatenate([b[0], b[1], b[2], b[0], b[1], b[0]], axis=0)
    return jnp.dot(left, right, preferred_element_type=jnp.float32)


def added_up(products, height, width):
    block = lambda i, j: products[i * height : (i + 1) * height, j * width : (j + 1) * width]
    small = (block(2, 2) + (block(1, 2) + block(2, 1))) + (block(0, 2) + block(2, 0) + block(1, 1))
    return small + (block(0, 1) + block(1, 0)) + block(0, 0)


def passed_along(shard, axis, by):
    peers = lax.axis_size(axis)
    return lax.ppermute(shard, axis, [(i, (i + by) % peers) for i in range(peers)])


def turn_kernel(total_rows, cross, side_ref, sums_ref, *refs):
    if cross:
        gram_stay_ref, gram_arrived_ref, gram_ref, turn_ref = refs
    else:
        gram_ref, turn_ref = refs
    order = gram_ref.shape[0]
    width = order // 2
    total = sums_ref[0]
    for device in range(1, sums_ref.shape[0]):
        total = total + sums_ref[device]
    if cross:
        block = jnp.concatenate([total[:, :width], total[:, width:]], axis=0)
        gram_ref[:width, :width] = gram_stay_ref[...]
        gram_ref[:width, width:] = block
        gram_ref[width:, :width] = block.T
        gram_ref[width:, width:] = gram_arrived_ref[...]
    else:
        gram_ref[:width, :] = total[:width]
        gram_ref[width:, :width] = total[:width, width:].T
        gram_ref[width:, width:] = jnp.concatenate([total[width:, :width], total[width:, width:]], axis=0)
    gram = gram_ref[...]
    scale = jnp.sqrt(jnp.sum(gram * gram) + 1e-06)
    down = lax.broadcasted_iota(jnp.int32, (order, order), 0)
    along = lax.broadcasted_iota(jnp.int32, (order, order), 1)
    half_more = jnp.where(down == along, 1.5, 0.0).astype(jnp.float32)
    ymat = gram / scale
    stepper = half_more - 0.5 * ymat
    beside = lambda y, z: [jnp.concatenate(pair, axis=1) for pair in zip(y, z)]
    z_terms = terms(stepper)
    y_terms = terms(mul_terms(z_terms, terms(ymat)))
    for step in range(1, NS_STEPS):
        stepper = half_more - 0.5 * mul_terms(z_terms, y_terms)
        if step + 1 < NS_STEPS:
            both = mul_terms(terms(stepper), beside(y_terms, z_terms))
            y_terms, z_terms = terms(both[:, :order]), terms(both[:, order:])
        else:
            zmat = mul_terms(terms(stepper), z_terms)
    zmat = zmat * jnp.sqrt(total_rows / scale)
    swapped = pltpu.roll(zmat, width, 0)
    turn_ref[...] = jnp.where(side_ref[0] == 0, zmat, swapped)


def turned(sums, side, total_rows, blocks=()):
    order = sums.shape[-1]
    square = jax.ShapeDtypeStruct((order, order), jnp.float32)
    return pl.pallas_call(
        functools.partial(turn_kernel, total_rows, bool(blocks)),
        out_shape=(square, square),
        in_specs=[pl.BlockSpec(memory_space=pltpu.SMEM)] + [IN_VMEM] * (1 + len(blocks)),
        out_specs=(IN_VMEM, IN_VMEM),
        compiler_params=pltpu.CompilerParams(vmem_limit_bytes=4 << 20),
        cost_estimate=pl.CostEstimate(flops=200_000_000, bytes_accessed=500_000, transcendentals=0),
    )(side, sums, *blocks)


def shares(copies):
    return lax.all_to_all(copies, "row", 0, 0)


def shares_of_chips(part):
    peers = lax.axis_size("row")
    part = part + lax.ppermute(part, "row", [(i, i ^ 1) for i in range(peers)])
    groups = [[core + 2 * chip for chip in range(peers // 2)] for core in range(2)]
    copies = jnp.broadcast_to(part[None], (peers // 2,) + part.shape)
    return lax.all_to_all(copies, "row", 0, 0, axis_index_groups=groups)


def folded(block):
    half = block.shape[0] // 2
    return jnp.concatenate([block[:half], block[half:]], axis=1)


def packed_gram(gram):
    width = gram.shape[0] // 2
    return jnp.concatenate([gram[:width], folded(gram[width:, width:])], axis=0)


def mul_nt(a, b):
    return lax.dot_general(a, b, (((1,), (1,)), ((), ())), precision=HIGHEST, preferred_element_type=jnp.float32)


def entry_kernel(x_ref, *refs):
    part_ref, xt_refs = refs[-1], refs[:-1]
    pieces = 8
    height = x_ref.shape[0] // pieces
    each = pieces // len(xt_refs)
    gram = None
    for piece in range(pieces):
        slab = x_ref[piece * height : (piece + 1) * height, :]
        turned_over = slab.T
        start = piece % each * height
        xt_refs[piece // each][:, start : start + height] = turned_over
        product = jnp.dot(
            jnp.concatenate(terms(turned_over), axis=0),
            jnp.concatenate(terms(slab), axis=1),
            preferred_element_type=jnp.float32,
        )
        gram = product if gram is None else gram + product
    part_ref[...] = packed_gram(added_up(gram, gram.shape[0] // 3, gram.shape[1] // 3))


def entry(matrix):
    rows, order = matrix.shape
    return pl.pallas_call(
        entry_kernel,
        out_shape=[jax.ShapeDtypeStruct((order, rows // GROUPS), jnp.float32)] * GROUPS
        + [jax.ShapeDtypeStruct((3 * order // 4, order), jnp.float32)],
        in_specs=[IN_VMEM],
        out_specs=[IN_VMEM] * (GROUPS + 1),
        compiler_params=pltpu.CompilerParams(vmem_limit_bytes=10 << 20),
        cost_estimate=pl.CostEstimate(flops=800_000_000, bytes_accessed=4_000_000, transcendentals=0),
    )(matrix)


def products(stay_ref, arrived_ref, whole):
    rows = stay_ref.shape[1]
    pieces = 2
    length = rows // pieces
    total = None
    for piece in range(pieces):
        where = slice(piece * length, (piece + 1) * length)
        left, right = stay_ref[:, where], arrived_ref[:, where]
        if whole:
            left = right = jnp.concatenate([left, right], axis=0)
        left = jnp.concatenate(terms(left), axis=0)
        right = left if whole else jnp.concatenate(terms(right), axis=0)
        product = lax.dot_general(left, right, (((1,), (1,)), ((), ())), preferred_element_type=jnp.float32)
        total = product if total is None else total + product
    total = added_up(total, total.shape[0] // 3, total.shape[1] // 3)
    return packed_gram(total) if whole else folded(total)


def first_gram_kernel(whole, stay_ref, arrived_ref, part_ref):
    part_ref[...] = products(stay_ref, arrived_ref, whole)


def last_gram_kernel(whole, before_ref, stay_ref, arrived_ref, part_ref):
    part = before_ref[...] + products(stay_ref, arrived_ref, whole)
    if whole:
        part_ref[...] = part
    else:
        for device in range(part_ref.shape[0]):
            part_ref[device] = part


def gram_part(stays, arriveds, copies=None, beside=None):
    width = stays[0].shape[0]
    whole = copies is None
    part = jax.ShapeDtypeStruct((3 * width // 2 if whole else width // 2, 2 * width), jnp.float32)
    result = part if whole else jax.ShapeDtypeStruct((copies,) + part.shape, jnp.float32)
    options = dict(
        out_specs=IN_VMEM,
        compiler_params=pltpu.CompilerParams(vmem_limit_bytes=8 << 20),
        cost_estimate=pl.CostEstimate(flops=400_000_000, bytes_accessed=3_000_000, transcendentals=0),
    )
    first = pl.pallas_call(
        functools.partial(first_gram_kernel, whole), out_shape=part, in_specs=[IN_VMEM] * 2, **options
    )(stays[0], arriveds[0])
    if beside is not None:
        first, beside = lax.optimization_barrier((first, beside))
    result = pl.pallas_call(
        functools.partial(last_gram_kernel, whole), out_shape=result, in_specs=[IN_VMEM] * 3, **options
    )(first, stays[1], arriveds[1])
    return result, beside


def exit_kernel(group, *refs):
    stay_ref, arrived_ref, out_ref, held_ref, sems = refs[-5:]
    pieces = sems.shape[0]
    height = held_ref.shape[0] // pieces
    copies = []
    for piece in range(pieces):
        where = slice(piece * height, (piece + 1) * height)
        held_ref[where, :] = jnp.concatenate([stay_ref[:, where], arrived_ref[:, where]], axis=0).T
        copy = pltpu.make_async_copy(
            held_ref.at[pl.ds(piece * height, height)],
            out_ref.at[pl.ds(group * pieces * height + piece * height, height)],
            sems.at[piece],
        )
        copy.start()
        copies.append(copy)
    for copy in copies:
        copy.wait()


def assembled(stays, arriveds):
    width, rows = stays[0].shape
    pieces = 4
    whole = ()
    for group in range(GROUPS):
        whole = (
            pl.pallas_call(
                functools.partial(exit_kernel, group),
                out_shape=jax.ShapeDtypeStruct((rows * GROUPS, 2 * width), jnp.float32),
                in_specs=[pl.BlockSpec(memory_space=pltpu.HBM)] * len(whole) + [IN_VMEM, IN_VMEM],
                out_specs=pl.BlockSpec(memory_space=pltpu.HBM),
                scratch_shapes=[pltpu.VMEM((rows, 2 * width), jnp.float32), pltpu.SemaphoreType.DMA((pieces,))],
                input_output_aliases={0: 0} if whole else {},
                compiler_params=pltpu.CompilerParams(vmem_limit_bytes=8 << 20),
                cost_estimate=pl.CostEstimate(flops=0, bytes_accessed=2_000_000, transcendentals=0),
            )(*whole, stays[group], arriveds[group]),
        )
    return whole[0]


def local(matrix, stay_side):
    rows, width = matrix.shape[0], matrix.shape[1] // 2
    total_rows = float(rows * lax.axis_size("row"))
    peers = lax.axis_size("row")
    *currents, part = entry(matrix)
    gram, turn = turned(shares_of_chips(part), stay_side[0], total_rows)
    for round_index in range(ROUNDS):
        following = round_index + 1
        to_stay, to_move = turn[:width], turn[width:]
        arriveds = [passed_along(mul(to_move, current), "pair", 1) for current in currents]
        stays = [mul(to_stay, current) for current in currents]
        if following == ROUNDS:
            return assembled(stays, arriveds)
        if following % 2 == 0:
            part, _ = gram_part(stays, arriveds)
            gram, turn = turned(shares_of_chips(part), stay_side[following], total_rows)
        else:
            gram_stay = mul_nt(mul(to_stay, gram), to_stay)
            gram_move = mul_nt(mul(to_move, gram), to_move)
            copies, gram_move = gram_part(stays, arriveds, peers, gram_move)
            gram_arrived = passed_along(gram_move, "pair", 1)
            gram, turn = turned(shares(copies), stay_side[following], total_rows, (gram_stay, gram_arrived))
        currents = [jnp.concatenate(pair, axis=0) for pair in zip(stays, arriveds)]


def solution(mesh):
    return jax.shard_map(
        local,
        mesh=mesh,
        in_specs=(P("row", "pair"), P(None, "pair")),
        out_specs=P("row", "pair"),
        check_vma=False,
    )
```

```python
import functools

import jax
import jax.numpy as jnp
from jax import lax
from jax.experimental import pallas as pl
from jax.experimental.pallas import tpu as pltpu
from jax.sharding import PartitionSpec as P

ROUNDS = 4
NS_STEPS = 6
GROUPS = 2
HIGHEST = lax.Precision.HIGHEST
IN_VMEM = pl.BlockSpec(memory_space=pltpu.VMEM)


def mul(a, b):
    return jnp.dot(a, b, precision=HIGHEST)


def terms(x):
    first = x.astype(jnp.bfloat16)
    rest = x - first.astype(jnp.float32)
    second = rest.astype(jnp.bfloat16)
    third = (rest - second.astype(jnp.float32)).astype(jnp.bfloat16)
    return first, second, third


def mul_terms(a, b):
    left = jnp.concatenate([a[0], a[0], a[0], a[1], a[1], a[2]], axis=1)
    right = jnp.concatenate([b[0], b[1], b[2], b[0], b[1], b[0]], axis=0)
    return jnp.dot(left, right, preferred_element_type=jnp.float32)


def added_up(products, height, width):
    block = lambda i, j: products[i * height : (i + 1) * height, j * width : (j + 1) * width]
    small = (block(2, 2) + (block(1, 2) + block(2, 1))) + (block(0, 2) + block(2, 0) + block(1, 1))
    return small + (block(0, 1) + block(1, 0)) + block(0, 0)


def passed_along(shard, axis, by):
    peers = lax.axis_size(axis)
    return lax.ppermute(shard, axis, [(i, (i + by) % peers) for i in range(peers)])


def turn_kernel(total_rows, cross, side_ref, sums_ref, *refs):
    if cross:
        gram_stay_ref, gram_arrived_ref, gram_ref, turn_ref = refs
    else:
        gram_ref, turn_ref = refs
    order = gram_ref.shape[0]
    width = order // 2
    total = sums_ref[0]
    for device in range(1, sums_ref.shape[0]):
        total = total + sums_ref[device]
    if cross:
        block = jnp.concatenate([total[:, :width], total[:, width:]], axis=0)
        gram_ref[:width, :width] = gram_stay_ref[...]
        gram_ref[:width, width:] = block
        gram_ref[width:, :width] = block.T
        gram_ref[width:, width:] = gram_arrived_ref[...]
    else:
        gram_ref[:width, :] = total[:width]
        gram_ref[width:, :width] = total[:width, width:].T
        gram_ref[width:, width:] = jnp.concatenate([total[width:, :width], total[width:, width:]], axis=0)
    gram = gram_ref[...]
    scale = jnp.sqrt(jnp.sum(gram * gram) + 1e-06)
    down = lax.broadcasted_iota(jnp.int32, (order, order), 0)
    along = lax.broadcasted_iota(jnp.int32, (order, order), 1)
    half_more = jnp.where(down == along, 1.5, 0.0).astype(jnp.float32)
    ymat = gram / scale
    stepper = half_more - 0.5 * ymat
    beside = lambda y, z: [jnp.concatenate(pair, axis=1) for pair in zip(y, z)]
    z_terms = terms(stepper)
    y_terms = terms(mul_terms(z_terms, terms(ymat)))
    for step in range(1, NS_STEPS):
        stepper = half_more - 0.5 * mul_terms(z_terms, y_terms)
        if step + 1 < NS_STEPS:
            both = mul_terms(terms(stepper), beside(y_terms, z_terms))
            y_terms, z_terms = terms(both[:, :order]), terms(both[:, order:])
        else:
            zmat = mul_terms(terms(stepper), z_terms)
    zmat = zmat * jnp.sqrt(total_rows / scale)
    swapped = pltpu.roll(zmat, width, 0)
    turn_ref[...] = jnp.where(side_ref[0] == 0, zmat, swapped)


def turned(sums, side, total_rows, blocks=()):
    order = sums.shape[-1]
    square = jax.ShapeDtypeStruct((order, order), jnp.float32)
    return pl.pallas_call(
        functools.partial(turn_kernel, total_rows, bool(blocks)),
        out_shape=(square, square),
        in_specs=[pl.BlockSpec(memory_space=pltpu.SMEM)] + [IN_VMEM] * (1 + len(blocks)),
        out_specs=(IN_VMEM, IN_VMEM),
        compiler_params=pltpu.CompilerParams(vmem_limit_bytes=4 << 20),
        cost_estimate=pl.CostEstimate(flops=200_000_000, bytes_accessed=500_000, transcendentals=0),
    )(side, sums, *blocks)


def shares(copies):
    return lax.all_to_all(copies, "row", 0, 0)


def shares_of_chips(part):
    peers = lax.axis_size("row")
    part = part + lax.ppermute(part, "row", [(i, i ^ 1) for i in range(peers)])
    groups = [[core + 2 * chip for chip in range(peers // 2)] for core in range(2)]
    copies = jnp.broadcast_to(part[None], (peers // 2,) + part.shape)
    return lax.all_to_all(copies, "row", 0, 0, axis_index_groups=groups)


def folded(block):
    half = block.shape[0] // 2
    return jnp.concatenate([block[:half], block[half:]], axis=1)


def packed_gram(gram):
    width = gram.shape[0] // 2
    return jnp.concatenate([gram[:width], folded(gram[width:, width:])], axis=0)


def mul_nt(a, b):
    return lax.dot_general(a, b, (((1,), (1,)), ((), ())), precision=HIGHEST, preferred_element_type=jnp.float32)


def entry_kernel(x_ref, *refs):
    part_ref, xt_refs = refs[-1], refs[:-1]
    pieces = 8
    height = x_ref.shape[0] // pieces
    each = pieces // GROUPS
    width = x_ref.shape[1] // 2
    gram = None
    for piece in range(pieces):
        slab = x_ref[piece * height : (piece + 1) * height, :]
        turned_over = slab.T
        start = piece % each * height
        xt_refs[piece // each][:, start : start + height] = turned_over[:width]
        xt_refs[GROUPS + piece // each][:, start : start + height] = turned_over[width:]
        product = jnp.dot(
            jnp.concatenate(terms(turned_over), axis=0),
            jnp.concatenate(terms(slab), axis=1),
            preferred_element_type=jnp.float32,
        )
        gram = product if gram is None else gram + product
    part_ref[...] = packed_gram(added_up(gram, gram.shape[0] // 3, gram.shape[1] // 3))


def entry(matrix):
    rows, order = matrix.shape
    return pl.pallas_call(
        entry_kernel,
        out_shape=[jax.ShapeDtypeStruct((order // 2, rows // GROUPS), jnp.float32)] * (2 * GROUPS)
        + [jax.ShapeDtypeStruct((3 * order // 4, order), jnp.float32)],
        in_specs=[IN_VMEM],
        out_specs=[IN_VMEM] * (2 * GROUPS + 1),
        compiler_params=pltpu.CompilerParams(vmem_limit_bytes=10 << 20),
        cost_estimate=pl.CostEstimate(flops=800_000_000, bytes_accessed=4_000_000, transcendentals=0),
    )(matrix)


def products(stay_ref, arrived_ref, whole):
    rows = stay_ref.shape[1]
    pieces = 2
    length = rows // pieces
    total = None
    for piece in range(pieces):
        where = slice(piece * length, (piece + 1) * length)
        left, right = stay_ref[:, where], arrived_ref[:, where]
        if whole:
            left = right = jnp.concatenate([left, right], axis=0)
        left = jnp.concatenate(terms(left), axis=0)
        right = left if whole else jnp.concatenate(terms(right), axis=0)
        product = lax.dot_general(left, right, (((1,), (1,)), ((), ())), preferred_element_type=jnp.float32)
        total = product if total is None else total + product
    total = added_up(total, total.shape[0] // 3, total.shape[1] // 3)
    return packed_gram(total) if whole else folded(total)


def first_gram_kernel(whole, stay_ref, arrived_ref, part_ref):
    part_ref[...] = products(stay_ref, arrived_ref, whole)


def last_gram_kernel(whole, before_ref, stay_ref, arrived_ref, part_ref):
    part = before_ref[...] + products(stay_ref, arrived_ref, whole)
    if whole:
        part_ref[...] = part
    else:
        for device in range(part_ref.shape[0]):
            part_ref[device] = part


def gram_part(stays, arriveds, copies=None, beside=None):
    width = stays[0].shape[0]
    whole = copies is None
    part = jax.ShapeDtypeStruct((3 * width // 2 if whole else width // 2, 2 * width), jnp.float32)
    result = part if whole else jax.ShapeDtypeStruct((copies,) + part.shape, jnp.float32)
    options = dict(
        out_specs=IN_VMEM,
        compiler_params=pltpu.CompilerParams(vmem_limit_bytes=8 << 20),
        cost_estimate=pl.CostEstimate(flops=400_000_000, bytes_accessed=3_000_000, transcendentals=0),
    )
    first = pl.pallas_call(
        functools.partial(first_gram_kernel, whole), out_shape=part, in_specs=[IN_VMEM] * 2, **options
    )(stays[0], arriveds[0])
    if beside is not None:
        first, beside = lax.optimization_barrier((first, beside))
    result = pl.pallas_call(
        functools.partial(last_gram_kernel, whole), out_shape=result, in_specs=[IN_VMEM] * 3, **options
    )(first, stays[1], arriveds[1])
    return result, beside


def exit_kernel(group, *refs):
    stay_ref, arrived_ref, out_ref, held_ref, sems = refs[-5:]
    pieces = sems.shape[0]
    height = held_ref.shape[0] // pieces
    copies = []
    for piece in range(pieces):
        where = slice(piece * height, (piece + 1) * height)
        held_ref[where, :] = jnp.concatenate([stay_ref[:, where], arrived_ref[:, where]], axis=0).T
        copy = pltpu.make_async_copy(
            held_ref.at[pl.ds(piece * height, height)],
            out_ref.at[pl.ds(group * pieces * height + piece * height, height)],
            sems.at[piece],
        )
        copy.start()
        copies.append(copy)
    for copy in copies:
        copy.wait()


def assembled(stays, arriveds):
    width, rows = stays[0].shape
    pieces = 4
    whole = ()
    for group in range(GROUPS):
        whole = (
            pl.pallas_call(
                functools.partial(exit_kernel, group),
                out_shape=jax.ShapeDtypeStruct((rows * GROUPS, 2 * width), jnp.float32),
                in_specs=[pl.BlockSpec(memory_space=pltpu.HBM)] * len(whole) + [IN_VMEM, IN_VMEM],
                out_specs=pl.BlockSpec(memory_space=pltpu.HBM),
                scratch_shapes=[pltpu.VMEM((rows, 2 * width), jnp.float32), pltpu.SemaphoreType.DMA((pieces,))],
                input_output_aliases={0: 0} if whole else {},
                compiler_params=pltpu.CompilerParams(vmem_limit_bytes=8 << 20),
                cost_estimate=pl.CostEstimate(flops=0, bytes_accessed=2_000_000, transcendentals=0),
            )(*whole, stays[group], arriveds[group]),
        )
    return whole[0]


def local(matrix, stay_side):
    rows, width = matrix.shape[0], matrix.shape[1] // 2
    total_rows = float(rows * lax.axis_size("row"))
    peers = lax.axis_size("row")
    *blocks, part = entry(matrix)
    currents = [jnp.concatenate(pair, axis=0) for pair in zip(blocks[:GROUPS], blocks[GROUPS:])]
    gram, turn = turned(shares_of_chips(part), stay_side[0], total_rows)
    for round_index in range(ROUNDS):
        following = round_index + 1
        to_stay, to_move = turn[:width], turn[width:]
        arriveds = [passed_along(mul(to_move, current), "pair", 1) for current in currents]
        stays = [mul(to_stay, current) for current in currents]
        if following == ROUNDS:
            return assembled(stays, arriveds)
        if following % 2 == 0:
            part, _ = gram_part(stays, arriveds)
            gram, turn = turned(shares_of_chips(part), stay_side[following], total_rows)
        else:
            gram_stay = mul_nt(mul(to_stay, gram), to_stay)
            gram_move = mul_nt(mul(to_move, gram), to_move)
            copies, gram_move = gram_part(stays, arriveds, peers, gram_move)
            gram_arrived = passed_along(gram_move, "pair", 1)
            gram, turn = turned(shares(copies), stay_side[following], total_rows, (gram_stay, gram_arrived))
        currents = [jnp.concatenate(pair, axis=0) for pair in zip(stays, arriveds)]


def solution(mesh):
    return jax.shard_map(
        local,
        mesh=mesh,
        in_specs=(P("row", "pair"), P(None, "pair")),
        out_specs=P("row", "pair"),
        check_vma=False,
    )
```

```python
import functools

import jax
import jax.numpy as jnp
from jax import lax
from jax.experimental import pallas as pl
from jax.experimental.pallas import tpu as pltpu
from jax.sharding import PartitionSpec as P

ROUNDS = 4
NS_STEPS = 6
GROUPS = 2
HIGHEST = lax.Precision.HIGHEST
IN_VMEM = pl.BlockSpec(memory_space=pltpu.VMEM)


def mul(a, b):
    return jnp.dot(a, b, precision=HIGHEST)


def terms(x):
    first = x.astype(jnp.bfloat16)
    rest = x - first.astype(jnp.float32)
    second = rest.astype(jnp.bfloat16)
    third = (rest - second.astype(jnp.float32)).astype(jnp.bfloat16)
    return first, second, third


def mul_terms(a, b):
    left = jnp.concatenate([a[0], a[0], a[0], a[1], a[1], a[2]], axis=1)
    right = jnp.concatenate([b[0], b[1], b[2], b[0], b[1], b[0]], axis=0)
    return jnp.dot(left, right, preferred_element_type=jnp.float32)


def added_up(products, height, width):
    block = lambda i, j: products[i * height : (i + 1) * height, j * width : (j + 1) * width]
    small = (block(2, 2) + (block(1, 2) + block(2, 1))) + (block(0, 2) + block(2, 0) + block(1, 1))
    return small + (block(0, 1) + block(1, 0)) + block(0, 0)


def passed_along(shard, axis, by):
    peers = lax.axis_size(axis)
    return lax.ppermute(shard, axis, [(i, (i + by) % peers) for i in range(peers)])


def turn_kernel(total_rows, cross, side_ref, sums_ref, *refs):
    if cross:
        gram_stay_ref, gram_arrived_ref, gram_ref, turn_ref = refs
    else:
        gram_ref, turn_ref = refs
    order = gram_ref.shape[0]
    width = order // 2
    total = sums_ref[0]
    for device in range(1, sums_ref.shape[0]):
        total = total + sums_ref[device]
    if cross:
        block = jnp.concatenate([total[:, :width], total[:, width:]], axis=0)
        gram_ref[:width, :width] = gram_stay_ref[...]
        gram_ref[:width, width:] = block
        gram_ref[width:, :width] = block.T
        gram_ref[width:, width:] = gram_arrived_ref[...]
    else:
        gram_ref[:width, :] = total[:width]
        gram_ref[width:, :width] = total[:width, width:].T
        gram_ref[width:, width:] = jnp.concatenate([total[width:, :width], total[width:, width:]], axis=0)
    gram = gram_ref[...]
    scale = jnp.sqrt(jnp.sum(gram * gram) + 1e-06)
    down = lax.broadcasted_iota(jnp.int32, (order, order), 0)
    along = lax.broadcasted_iota(jnp.int32, (order, order), 1)
    half_more = jnp.where(down == along, 1.5, 0.0).astype(jnp.float32)
    ymat = gram / scale
    stepper = half_more - 0.5 * ymat
    beside = lambda y, z: [jnp.concatenate(pair, axis=1) for pair in zip(y, z)]
    z_terms = terms(stepper)
    y_terms = terms(mul_terms(z_terms, terms(ymat)))
    for step in range(1, NS_STEPS):
        stepper = half_more - 0.5 * mul_terms(z_terms, y_terms)
        if step + 1 < NS_STEPS:
            both = mul_terms(terms(stepper), beside(y_terms, z_terms))
            y_terms, z_terms = terms(both[:, :order]), terms(both[:, order:])
        else:
            zmat = mul_terms(terms(stepper), z_terms)
    zmat = zmat * jnp.sqrt(total_rows / scale)
    swapped = pltpu.roll(zmat, width, 0)
    turn_ref[...] = jnp.where(side_ref[0] == 0, zmat, swapped)


def turned(sums, side, total_rows, blocks=()):
    order = sums.shape[-1]
    square = jax.ShapeDtypeStruct((order, order), jnp.float32)
    return pl.pallas_call(
        functools.partial(turn_kernel, total_rows, bool(blocks)),
        out_shape=(square, square),
        in_specs=[pl.BlockSpec(memory_space=pltpu.SMEM)] + [IN_VMEM] * (1 + len(blocks)),
        out_specs=(IN_VMEM, IN_VMEM),
        compiler_params=pltpu.CompilerParams(vmem_limit_bytes=4 << 20),
        cost_estimate=pl.CostEstimate(flops=200_000_000, bytes_accessed=500_000, transcendentals=0),
    )(side, sums, *blocks)


def shares(copies):
    return lax.all_to_all(copies, "row", 0, 0)


def shares_of_chips(part):
    peers = lax.axis_size("row")
    part = part + lax.ppermute(part, "row", [(i, i ^ 1) for i in range(peers)])
    groups = [[core + 2 * chip for chip in range(peers // 2)] for core in range(2)]
    copies = jnp.broadcast_to(part[None], (peers // 2,) + part.shape)
    return lax.all_to_all(copies, "row", 0, 0, axis_index_groups=groups)


def folded(block):
    half = block.shape[0] // 2
    return jnp.concatenate([block[:half], block[half:]], axis=1)


def packed_gram(gram):
    width = gram.shape[0] // 2
    return jnp.concatenate([gram[:width], folded(gram[width:, width:])], axis=0)


def mul_nt(a, b):
    return lax.dot_general(a, b, (((1,), (1,)), ((), ())), precision=HIGHEST, preferred_element_type=jnp.float32)


def entry_kernel(x_ref, *refs):
    part_ref, xt_refs = refs[-1], refs[:-1]
    pieces = 8
    height = x_ref.shape[0] // pieces
    each = pieces // GROUPS
    width = x_ref.shape[1] // 2
    gram = None
    for piece in range(pieces):
        slab = x_ref[piece * height : (piece + 1) * height, :]
        turned_over = slab.T
        start = piece % each * height
        xt_refs[piece // each][:, start : start + height] = turned_over[:width]
        xt_refs[GROUPS + piece // each][:, start : start + height] = turned_over[width:]
        product = jnp.dot(
            jnp.concatenate(terms(turned_over), axis=0),
            jnp.concatenate(terms(slab), axis=1),
            preferred_element_type=jnp.float32,
        )
        gram = product if gram is None else gram + product
    part_ref[...] = packed_gram(added_up(gram, gram.shape[0] // 3, gram.shape[1] // 3))


def entry(matrix):
    rows, order = matrix.shape
    return pl.pallas_call(
        entry_kernel,
        out_shape=[jax.ShapeDtypeStruct((order // 2, rows // GROUPS), jnp.float32)] * (2 * GROUPS)
        + [jax.ShapeDtypeStruct((3 * order // 4, order), jnp.float32)],
        in_specs=[IN_VMEM],
        out_specs=[IN_VMEM] * (2 * GROUPS + 1),
        compiler_params=pltpu.CompilerParams(vmem_limit_bytes=10 << 20),
        cost_estimate=pl.CostEstimate(flops=800_000_000, bytes_accessed=4_000_000, transcendentals=0),
    )(matrix)


def products(stay_ref, arrived_ref, whole):
    rows = stay_ref.shape[1]
    pieces = 2
    length = rows // pieces
    total = None
    for piece in range(pieces):
        where = slice(piece * length, (piece + 1) * length)
        left, right = stay_ref[:, where], arrived_ref[:, where]
        if whole:
            left = right = jnp.concatenate([left, right], axis=0)
        left = jnp.concatenate(terms(left), axis=0)
        right = left if whole else jnp.concatenate(terms(right), axis=0)
        product = lax.dot_general(left, right, (((1,), (1,)), ((), ())), preferred_element_type=jnp.float32)
        total = product if total is None else total + product
    total = added_up(total, total.shape[0] // 3, total.shape[1] // 3)
    return packed_gram(total) if whole else folded(total)


def first_gram_kernel(whole, stay_ref, arrived_ref, part_ref):
    part_ref[...] = products(stay_ref, arrived_ref, whole)


def last_gram_kernel(before_ref, stay_ref, arrived_ref, part_ref):
    part_ref[...] = before_ref[...] + products(stay_ref, arrived_ref, True)


def last_cross_kernel(before_ref, stay_ref, arrived_ref, copies_ref, held_ref, sems):
    held_ref[...] = before_ref[...] + products(stay_ref, arrived_ref, False)
    copies = [
        pltpu.make_async_copy(held_ref, copies_ref.at[device], sems.at[device]) for device in range(sems.shape[0])
    ]
    for copy in copies:
        copy.start()
    for copy in copies:
        copy.wait()


def gram_part(stays, arriveds, copies=None, beside=None):
    width = stays[0].shape[0]
    whole = copies is None
    part = jax.ShapeDtypeStruct((3 * width // 2 if whole else width // 2, 2 * width), jnp.float32)
    result = part if whole else jax.ShapeDtypeStruct((copies,) + part.shape, jnp.float32)
    options = dict(
        compiler_params=pltpu.CompilerParams(vmem_limit_bytes=8 << 20),
        cost_estimate=pl.CostEstimate(flops=400_000_000, bytes_accessed=3_000_000, transcendentals=0),
    )
    first = pl.pallas_call(
        functools.partial(first_gram_kernel, whole), out_shape=part, in_specs=[IN_VMEM] * 2, out_specs=IN_VMEM, **options
    )(stays[0], arriveds[0])
    if beside is not None:
        first, beside = lax.optimization_barrier((first, beside))
    if not whole:
        options["scratch_shapes"] = [pltpu.VMEM(part.shape, jnp.float32), pltpu.SemaphoreType.DMA((copies,))]
    result = pl.pallas_call(
        last_gram_kernel if whole else last_cross_kernel,
        out_shape=result,
        in_specs=[IN_VMEM] * 3,
        out_specs=IN_VMEM if whole else pl.BlockSpec(memory_space=pltpu.HBM),
        **options,
    )(first, stays[1], arriveds[1])
    return result, beside


def exit_kernel(group, *refs):
    stay_ref, arrived_ref, out_ref, held_ref, sems = refs[-5:]
    pieces = sems.shape[0]
    height = held_ref.shape[0] // pieces
    copies = []
    for piece in range(pieces):
        where = slice(piece * height, (piece + 1) * height)
        held_ref[where, :] = jnp.concatenate([stay_ref[:, where], arrived_ref[:, where]], axis=0).T
        copy = pltpu.make_async_copy(
            held_ref.at[pl.ds(piece * height, height)],
            out_ref.at[pl.ds(group * pieces * height + piece * height, height)],
            sems.at[piece],
        )
        copy.start()
        copies.append(copy)
    for copy in copies:
        copy.wait()


def assembled(stays, arriveds):
    width, rows = stays[0].shape
    pieces = 4
    whole = ()
    for group in range(GROUPS):
        whole = (
            pl.pallas_call(
                functools.partial(exit_kernel, group),
                out_shape=jax.ShapeDtypeStruct((rows * GROUPS, 2 * width), jnp.float32),
                in_specs=[pl.BlockSpec(memory_space=pltpu.HBM)] * len(whole) + [IN_VMEM, IN_VMEM],
                out_specs=pl.BlockSpec(memory_space=pltpu.HBM),
                scratch_shapes=[pltpu.VMEM((rows, 2 * width), jnp.float32), pltpu.SemaphoreType.DMA((pieces,))],
                input_output_aliases={0: 0} if whole else {},
                compiler_params=pltpu.CompilerParams(vmem_limit_bytes=8 << 20),
                cost_estimate=pl.CostEstimate(flops=0, bytes_accessed=2_000_000, transcendentals=0),
            )(*whole, stays[group], arriveds[group]),
        )
    return whole[0]


def local(matrix, stay_side):
    rows, width = matrix.shape[0], matrix.shape[1] // 2
    total_rows = float(rows * lax.axis_size("row"))
    peers = lax.axis_size("row")
    *blocks, part = entry(matrix)
    currents = [jnp.concatenate(pair, axis=0) for pair in zip(blocks[:GROUPS], blocks[GROUPS:])]
    gram, turn = turned(shares_of_chips(part), stay_side[0], total_rows)
    for round_index in range(ROUNDS):
        following = round_index + 1
        to_stay, to_move = turn[:width], turn[width:]
        arriveds = [passed_along(mul(to_move, current), "pair", 1) for current in currents]
        stays = [mul(to_stay, current) for current in currents]
        if following == ROUNDS:
            return assembled(stays, arriveds)
        if following % 2 == 0:
            part, _ = gram_part(stays, arriveds)
            gram, turn = turned(shares_of_chips(part), stay_side[following], total_rows)
        else:
            gram_stay = mul_nt(mul(to_stay, gram), to_stay)
            gram_move = mul_nt(mul(to_move, gram), to_move)
            copies, gram_move = gram_part(stays, arriveds, peers, gram_move)
            gram_arrived = passed_along(gram_move, "pair", 1)
            gram, turn = turned(shares(copies), stay_side[following], total_rows, (gram_stay, gram_arrived))
        currents = [jnp.concatenate(pair, axis=0) for pair in zip(stays, arriveds)]


def solution(mesh):
    return jax.shard_map(
        local,
        mesh=mesh,
        in_specs=(P("row", "pair"), P(None, "pair")),
        out_specs=P("row", "pair"),
        check_vma=False,
    )
```

```python
import functools

import jax
import jax.numpy as jnp
from jax import lax
from jax.experimental import pallas as pl
from jax.experimental.pallas import tpu as pltpu
from jax.sharding import PartitionSpec as P

ROUNDS = 4
NS_STEPS = 6
GROUPS = 2
HIGHEST = lax.Precision.HIGHEST
IN_VMEM = pl.BlockSpec(memory_space=pltpu.VMEM)


def mul(a, b):
    return jnp.dot(a, b, precision=HIGHEST)


def terms(x):
    first = x.astype(jnp.bfloat16)
    rest = x - first.astype(jnp.float32)
    second = rest.astype(jnp.bfloat16)
    third = (rest - second.astype(jnp.float32)).astype(jnp.bfloat16)
    return first, second, third


def mul_terms(a, b):
    left = jnp.concatenate([a[0], a[0], a[0], a[1], a[1], a[2]], axis=1)
    right = jnp.concatenate([b[0], b[1], b[2], b[0], b[1], b[0]], axis=0)
    return jnp.dot(left, right, preferred_element_type=jnp.float32)


def added_up(products, height, width):
    block = lambda i, j: products[i * height : (i + 1) * height, j * width : (j + 1) * width]
    small = (block(2, 2) + (block(1, 2) + block(2, 1))) + (block(0, 2) + block(2, 0) + block(1, 1))
    return small + (block(0, 1) + block(1, 0)) + block(0, 0)


def passed_along(shard, axis, by):
    peers = lax.axis_size(axis)
    return lax.ppermute(shard, axis, [(i, (i + by) % peers) for i in range(peers)])


def turn_kernel(total_rows, cross, side_ref, sums_ref, *refs):
    if cross:
        gram_stay_ref, gram_arrived_ref, gram_ref, turn_ref = refs
    else:
        gram_ref, turn_ref = refs
    order = gram_ref.shape[0]
    width = order // 2
    total = sums_ref[0]
    for device in range(1, sums_ref.shape[0]):
        total = total + sums_ref[device]
    if cross:
        block = jnp.concatenate([total[:, :width], total[:, width:]], axis=0)
        gram_ref[:width, :width] = gram_stay_ref[...]
        gram_ref[:width, width:] = block
        gram_ref[width:, :width] = block.T
        gram_ref[width:, width:] = gram_arrived_ref[...]
    else:
        gram_ref[:width, :] = total[:width]
        gram_ref[width:, :width] = total[:width, width:].T
        gram_ref[width:, width:] = jnp.concatenate([total[width:, :width], total[width:, width:]], axis=0)
    gram = gram_ref[...]
    scale = jnp.sqrt(jnp.sum(gram * gram) + 1e-06)
    down = lax.broadcasted_iota(jnp.int32, (order, order), 0)
    along = lax.broadcasted_iota(jnp.int32, (order, order), 1)
    half_more = jnp.where(down == along, 1.5, 0.0).astype(jnp.float32)
    ymat = gram / scale
    stepper = half_more - 0.5 * ymat
    beside = lambda y, z: [jnp.concatenate(pair, axis=1) for pair in zip(y, z)]
    z_terms = terms(stepper)
    y_terms = terms(mul_terms(z_terms, terms(ymat)))
    for step in range(1, NS_STEPS):
        stepper = half_more - 0.5 * mul_terms(z_terms, y_terms)
        if step + 1 < NS_STEPS:
            both = mul_terms(terms(stepper), beside(y_terms, z_terms))
            y_terms, z_terms = terms(both[:, :order]), terms(both[:, order:])
        else:
            zmat = mul_terms(terms(stepper), z_terms)
    zmat = zmat * jnp.sqrt(total_rows / scale)
    swapped = pltpu.roll(zmat, width, 0)
    turn_ref[...] = jnp.where(side_ref[0] == 0, zmat, swapped)


def turned(sums, side, total_rows, blocks=()):
    order = sums.shape[-1]
    square = jax.ShapeDtypeStruct((order, order), jnp.float32)
    return pl.pallas_call(
        functools.partial(turn_kernel, total_rows, bool(blocks)),
        out_shape=(square, square),
        in_specs=[pl.BlockSpec(memory_space=pltpu.SMEM)] + [IN_VMEM] * (1 + len(blocks)),
        out_specs=(IN_VMEM, IN_VMEM),
        compiler_params=pltpu.CompilerParams(vmem_limit_bytes=4 << 20),
        cost_estimate=pl.CostEstimate(flops=200_000_000, bytes_accessed=500_000, transcendentals=0),
    )(side, sums, *blocks)


def shares(copies):
    return lax.all_to_all(copies, "row", 0, 0)


def shares_of_chips(part):
    peers = lax.axis_size("row")
    part = part + lax.ppermute(part, "row", [(i, i ^ 1) for i in range(peers)])
    groups = [[core + 2 * chip for chip in range(peers // 2)] for core in range(2)]
    copies = jnp.broadcast_to(part[None], (peers // 2,) + part.shape)
    return lax.all_to_all(copies, "row", 0, 0, axis_index_groups=groups)


def folded(block):
    half = block.shape[0] // 2
    return jnp.concatenate([block[:half], block[half:]], axis=1)


def packed_gram(gram):
    width = gram.shape[0] // 2
    return jnp.concatenate([gram[:width], folded(gram[width:, width:])], axis=0)


def mul_nt(a, b):
    return lax.dot_general(a, b, (((1,), (1,)), ((), ())), precision=HIGHEST, preferred_element_type=jnp.float32)


def entry_kernel(x_ref, *refs):
    part_ref, xt_refs = refs[-1], refs[:-1]
    pieces = 4
    height = x_ref.shape[0] // pieces
    each = pieces // GROUPS
    width = x_ref.shape[1] // 2
    gram = None
    for piece in range(pieces):
        slab = x_ref[piece * height : (piece + 1) * height, :]
        turned_over = slab.T
        start = piece % each * height
        xt_refs[piece // each][:, start : start + height] = turned_over[:width]
        xt_refs[GROUPS + piece // each][:, start : start + height] = turned_over[width:]
        product = jnp.dot(
            jnp.concatenate(terms(turned_over), axis=0),
            jnp.concatenate(terms(slab), axis=1),
            preferred_element_type=jnp.float32,
        )
        gram = product if gram is None else gram + product
    part_ref[...] = packed_gram(added_up(gram, gram.shape[0] // 3, gram.shape[1] // 3))


def entry(matrix):
    rows, order = matrix.shape
    return pl.pallas_call(
        entry_kernel,
        out_shape=[jax.ShapeDtypeStruct((order // 2, rows // GROUPS), jnp.float32)] * (2 * GROUPS)
        + [jax.ShapeDtypeStruct((3 * order // 4, order), jnp.float32)],
        in_specs=[IN_VMEM],
        out_specs=[IN_VMEM] * (2 * GROUPS + 1),
        compiler_params=pltpu.CompilerParams(vmem_limit_bytes=10 << 20),
        cost_estimate=pl.CostEstimate(flops=800_000_000, bytes_accessed=4_000_000, transcendentals=0),
    )(matrix)


def products(stay_ref, arrived_ref, whole):
    rows = stay_ref.shape[1]
    pieces = 1
    length = rows // pieces
    total = None
    for piece in range(pieces):
        where = slice(piece * length, (piece + 1) * length)
        left, right = stay_ref[:, where], arrived_ref[:, where]
        if whole:
            left = right = jnp.concatenate([left, right], axis=0)
        left = jnp.concatenate(terms(left), axis=0)
        right = left if whole else jnp.concatenate(terms(right), axis=0)
        product = lax.dot_general(left, right, (((1,), (1,)), ((), ())), preferred_element_type=jnp.float32)
        total = product if total is None else total + product
    total = added_up(total, total.shape[0] // 3, total.shape[1] // 3)
    return packed_gram(total) if whole else folded(total)


def first_gram_kernel(whole, stay_ref, arrived_ref, part_ref):
    part_ref[...] = products(stay_ref, arrived_ref, whole)


def last_gram_kernel(whole, before_ref, stay_ref, arrived_ref, part_ref):
    part = before_ref[...] + products(stay_ref, arrived_ref, whole)
    if whole:
        part_ref[...] = part
    else:
        for device in range(part_ref.shape[0]):
            part_ref[device] = part


def gram_part(stays, arriveds, copies=None, beside=None):
    width = stays[0].shape[0]
    whole = copies is None
    part = jax.ShapeDtypeStruct((3 * width // 2 if whole else width // 2, 2 * width), jnp.float32)
    result = part if whole else jax.ShapeDtypeStruct((copies,) + part.shape, jnp.float32)
    options = dict(
        out_specs=IN_VMEM,
        compiler_params=pltpu.CompilerParams(vmem_limit_bytes=8 << 20),
        cost_estimate=pl.CostEstimate(flops=400_000_000, bytes_accessed=3_000_000, transcendentals=0),
    )
    first = pl.pallas_call(
        functools.partial(first_gram_kernel, whole), out_shape=part, in_specs=[IN_VMEM] * 2, **options
    )(stays[0], arriveds[0])
    if beside is not None:
        first, beside = lax.optimization_barrier((first, beside))
    result = pl.pallas_call(
        functools.partial(last_gram_kernel, whole), out_shape=result, in_specs=[IN_VMEM] * 3, **options
    )(first, stays[1], arriveds[1])
    return result, beside


def exit_kernel(group, *refs):
    stay_ref, arrived_ref, out_ref, held_ref, sems = refs[-5:]
    pieces = sems.shape[0]
    height = held_ref.shape[0] // pieces
    copies = []
    for piece in range(pieces):
        where = slice(piece * height, (piece + 1) * height)
        held_ref[where, :] = jnp.concatenate([stay_ref[:, where], arrived_ref[:, where]], axis=0).T
        copy = pltpu.make_async_copy(
            held_ref.at[pl.ds(piece * height, height)],
            out_ref.at[pl.ds(group * pieces * height + piece * height, height)],
            sems.at[piece],
        )
        copy.start()
        copies.append(copy)
    for copy in copies:
        copy.wait()


def assembled(stays, arriveds):
    width, rows = stays[0].shape
    pieces = 4
    whole = ()
    for group in range(GROUPS):
        whole = (
            pl.pallas_call(
                functools.partial(exit_kernel, group),
                out_shape=jax.ShapeDtypeStruct((rows * GROUPS, 2 * width), jnp.float32),
                in_specs=[pl.BlockSpec(memory_space=pltpu.HBM)] * len(whole) + [IN_VMEM, IN_VMEM],
                out_specs=pl.BlockSpec(memory_space=pltpu.HBM),
                scratch_shapes=[pltpu.VMEM((rows, 2 * width), jnp.float32), pltpu.SemaphoreType.DMA((pieces,))],
                input_output_aliases={0: 0} if whole else {},
                compiler_params=pltpu.CompilerParams(vmem_limit_bytes=8 << 20),
                cost_estimate=pl.CostEstimate(flops=0, bytes_accessed=2_000_000, transcendentals=0),
            )(*whole, stays[group], arriveds[group]),
        )
    return whole[0]


def local(matrix, stay_side):
    rows, width = matrix.shape[0], matrix.shape[1] // 2
    total_rows = float(rows * lax.axis_size("row"))
    peers = lax.axis_size("row")
    *blocks, part = entry(matrix)
    currents = [jnp.concatenate(pair, axis=0) for pair in zip(blocks[:GROUPS], blocks[GROUPS:])]
    gram, turn = turned(shares_of_chips(part), stay_side[0], total_rows)
    for round_index in range(ROUNDS):
        following = round_index + 1
        to_stay, to_move = turn[:width], turn[width:]
        arriveds = [passed_along(mul(to_move, current), "pair", 1) for current in currents]
        stays = [mul(to_stay, current) for current in currents]
        if following == ROUNDS:
            return assembled(stays, arriveds)
        if following % 2 == 0:
            part, _ = gram_part(stays, arriveds)
            gram, turn = turned(shares_of_chips(part), stay_side[following], total_rows)
        else:
            gram_stay = mul_nt(mul(to_stay, gram), to_stay)
            gram_move = mul_nt(mul(to_move, gram), to_move)
            copies, gram_move = gram_part(stays, arriveds, peers, gram_move)
            gram_arrived = passed_along(gram_move, "pair", 1)
            gram, turn = turned(shares(copies), stay_side[following], total_rows, (gram_stay, gram_arrived))
        currents = [jnp.concatenate(pair, axis=0) for pair in zip(stays, arriveds)]


def solution(mesh):
    return jax.shard_map(
        local,
        mesh=mesh,
        in_specs=(P("row", "pair"), P(None, "pair")),
        out_specs=P("row", "pair"),
        check_vma=False,
    )
```
